256 devices in a mesh: inner: 8 (over z_lo, y), outer: 32 (over z_hi, x, core).
Axes of the slice: x: 4, y: 4, z: 8 (z_hi: 4, z_lo: 2; z = z_hi * 2 + z_lo), core: 2. Of those that a mesh axis runs over, the one named last changes fastest.
Arguments:
- queries: bfloat16 [32768, 2048], P(('outer', 'inner')), may hold values from -5 to 5, as said below
- keys: bfloat16 [32768, 2048], P(('outer', 'inner')), may hold values from -5 to 5, as said below
- values: bfloat16 [32768, 2048], P(('outer', 'inner')), may hold values from -6 to 6
- out_grad: bfloat16 [32768, 2048], P(('outer', 'inner')), may hold values from -6 to 6
- stretch_pos: int32 [512], replicated, may hold values from 0 to 511, as said below
- block_mask: int32 [512, 32], replicated, may hold values from 0 to 1, as said below
Outputs:
- attn_out: bfloat16 [32768, 2048], P(('outer', 'inner'))
- d_query: bfloat16 [32768, 2048], P(('outer', 'inner'))
- d_key: bfloat16 [32768, 2048], P(('outer', 'inner'))
- d_value: bfloat16 [32768, 2048], P(('outer', 'inner'))
The draws below stay inside these ranges and needn't reach their ends.
Inputs may be any that keep to these rules, and one draw needn't show every extreme that they name: `queries`: a query row's features lie in the printed range. `keys`: a key row's features lie in the printed range. `stretch_pos`: paired order: stored stretches 2 g and 2 g + 1 hold sequence stretches p and 511 - p for some p below 256; every stretch position appears once. `block_mask`: each stretch's entry for itself (window index c mod (16)) is 1.
All inputs are finite; a program needn't handle non-finite values.
Results may differ from the reference program's by a relative error of at most 0.027.
Values may be sent and summed in bfloat16 or wider, within the bound.
No kernel may reach another device: no remote copies, remote signals or barrier semaphores. Data moves between devices by JAX's collectives and lax.ppermute only.
A program may use at most 128 MiB of HBM per device.

```python
import jax
import jax.numpy as jnp
from jax import lax

H = 16
HEAD = 128
TOK_DEV = 128
HD = 2048
CH = 64
NCH = 512
WIN = 32
TOKENS = 32768
N_INNER = 8
N_OUTER = 32
DEVICES = 256


def draw_queries(key, part):
    key = jax.random.fold_in(key, 1)
    drawn = jnp.clip(jax.random.normal(key, (TOKENS, HD), jnp.float32), -4.5, 4.5)
    return drawn.astype(jnp.bfloat16)


def draw_keys(key, part):
    key = jax.random.fold_in(key, 2)
    drawn = jnp.clip(jax.random.normal(key, (TOKENS, HD), jnp.float32), -4.5, 4.5)
    return drawn.astype(jnp.bfloat16)


def draw_stretch_pos(key, part):
    key = jax.random.fold_in(key, 3)
    order = jax.random.permutation(key, DEVICES).astype(jnp.int32)
    paired = jnp.stack([order, NCH - 1 - order], axis=1)
    return paired.reshape(NCH).astype(jnp.int32)


def draw_block_mask(key, part):
    key = jax.random.fold_in(key, 4)
    random_bits = (jax.random.randint(key, (NCH, WIN), 0, 4) > 0).astype(jnp.int32)
    rows_index = jnp.arange(NCH)[:, None]
    column_index = jnp.arange(WIN)[None, :]
    itself = column_index == rows_index % (WIN // 2)
    return jnp.where(itself, 1, random_bits).astype(jnp.int32)


def level_of(key, extent, split, least, largest):
    factor_of, own = 1.0, jax.random.fold_in(key, 6)
    for dim, parts in split:
        draws = jnp.exp(jax.random.uniform(jax.random.fold_in(own, dim), (parts,), jnp.float32, least / len(split), largest / len(split)))
        factor_of = factor_of * jnp.repeat(draws, extent[dim] // parts).reshape([-1 if axis == dim else 1 for axis in range(len(extent))])
    return factor_of


def normal_values(stream_key, dims, scale, limit, shards=(), kind=jnp.bfloat16):
    level = level_of(stream_key, dims, shards, -0.22, 0.18) if shards else 1.0
    values = jax.random.normal(stream_key, dims, jnp.float32) * scale * level
    return jnp.minimum(jnp.maximum(values, -limit), limit).astype(kind)


def setup_inputs(seed: int = 0) -> dict:
    streams_of = jax.random.split(jax.random.key(seed), 7)
    return {
        "queries": draw_queries(jax.random.fold_in(streams_of[6], 71), 0),
        "keys": draw_keys(jax.random.fold_in(streams_of[6], 71), 0),
        "values": normal_values(streams_of[2], (TOKENS, HD), 1.0, 6.0, ((0, 256),)),
        "out_grad": normal_values(streams_of[3], (TOKENS, HD), 1.0, 6.0, ((0, 256),)),
        "stretch_pos": draw_stretch_pos(jax.random.fold_in(streams_of[6], 71), 0),
        "block_mask": draw_block_mask(jax.random.fold_in(streams_of[6], 71), 0),
    }


def window_mask(query_pos, key_pos, flags):
    seen = flags[:, None, :, None] == 1
    causal = key_pos[None, None, :, :] <= query_pos[:, :, None, None]
    both = jnp.logical_and(seen, causal)
    return both.reshape(query_pos.shape[0] * query_pos.shape[1], key_pos.shape[0] * key_pos.shape[1])


def device_attention(query, window_k, window_v, out_grad, allowed):
    rows = query.shape[0]
    width = window_k.shape[0]
    scale = 1.0 / (HEAD ** 0.5)
    query3 = query.reshape(rows, H, HEAD).astype(jnp.float32)
    key3 = window_k.reshape(width, H, HEAD).astype(jnp.float32)
    value3 = window_v.reshape(width, H, HEAD).astype(jnp.float32)
    grad3 = out_grad.reshape(rows, H, HEAD).astype(jnp.float32)
    scores = jnp.einsum("qhd,khd->hqk", query3, key3) * scale
    masked = jnp.where(allowed[None], scores, -1e30)
    top = jnp.max(masked, axis=-1, keepdims=True)
    expo = jnp.where(allowed[None], jnp.exp(masked - top), 0.0)
    probs = expo / jnp.sum(expo, axis=-1, keepdims=True)
    probs_b = probs.astype(jnp.bfloat16)
    output = jnp.einsum("hqk,khd->qhd", probs_b.astype(jnp.float32), value3).astype(jnp.bfloat16)
    delta = jnp.sum(grad3 * output.astype(jnp.float32), axis=-1)
    dprob = jnp.einsum("qhd,khd->hqk", grad3, value3)
    dscore = (probs * (dprob - jnp.transpose(delta)[:, :, None])).astype(jnp.bfloat16)
    dscore32 = dscore.astype(jnp.float32)
    dquery = (jnp.einsum("hqk,khd->qhd", dscore32, key3) * scale).astype(jnp.bfloat16)
    dkey = jnp.einsum("hqk,qhd->khd", dscore32, query3) * scale
    dvalue = jnp.einsum("hqk,qhd->khd", probs_b.astype(jnp.float32), grad3)
    return (output.reshape(rows, HD), dquery.reshape(rows, HD), dkey.reshape(width, HD), dvalue.reshape(width, HD))


def group_sum(terms):
    rounded = lax.optimization_barrier(terms.astype(jnp.bfloat16))
    return jnp.sum(rounded.astype(jnp.float32), axis=0).astype(jnp.bfloat16)


def reference(queries, keys, values, out_grad, stretch_pos, block_mask):
    offsets = jnp.arange(CH, dtype=jnp.int32)
    pos_rows = stretch_pos[:, None] * CH + offsets[None, :]
    pos_group = pos_rows.reshape(N_OUTER, 2 * N_INNER, CH)
    key_pos = jnp.concatenate([pos_group, jnp.roll(pos_group, 1, axis=0)], axis=1)
    query_pos = pos_group.reshape(N_OUTER, N_INNER, 2, CH)
    flags = block_mask.reshape(N_OUTER, N_INNER, 2, WIN)
    key_group = keys.reshape(N_OUTER, N_INNER * TOK_DEV, HD)
    value_group = values.reshape(N_OUTER, N_INNER * TOK_DEV, HD)
    window_k = jnp.concatenate([key_group, jnp.roll(key_group, 1, axis=0)], axis=1)
    window_v = jnp.concatenate([value_group, jnp.roll(value_group, 1, axis=0)], axis=1)
    query_dev = queries.reshape(N_OUTER, N_INNER, TOK_DEV, HD)
    grad_dev = out_grad.reshape(N_OUTER, N_INNER, TOK_DEV, HD)

    def one_group(items):
        query_g, grad_g, win_k, win_v, qpos_g, kpos_g, flags_g = items

        def one_device(query, grad, qpos, flag):
            allowed = window_mask(qpos, kpos_g, flag)
            return device_attention(query, win_k, win_v, grad, allowed)

        output, dquery, dkey, dvalue = jax.vmap(one_device)(query_g, grad_g, qpos_g, flags_g)
        return output, dquery, group_sum(dkey), group_sum(dvalue)

    output, dquery, dkey, dvalue = lax.map(one_group, (query_dev, grad_dev, window_k, window_v, query_pos, key_pos, flags))
    span = N_INNER * TOK_DEV
    d_key = (dkey[:, :span].astype(jnp.float32) + jnp.roll(dkey[:, span:], -1, axis=0).astype(jnp.float32)).astype(jnp.bfloat16)
    d_value = (dvalue[:, :span].astype(jnp.float32) + jnp.roll(dvalue[:, span:], -1, axis=0).astype(jnp.float32)).astype(jnp.bfloat16)
    return (output.reshape(TOKENS, HD), dquery.reshape(TOKENS, HD), d_key.reshape(TOKENS, HD), d_value.reshape(TOKENS, HD))
```

```python
import functools

import jax
import jax.numpy as jnp
from jax import lax
from jax.experimental import pallas as pl
from jax.experimental.pallas import tpu as pltpu
from jax.sharding import PartitionSpec as P

H = 16
HEAD = 128
CH = 64
NEG = -1e30
TILE = 256
SCALE = 1.0 / HEAD**0.5
LOG2E = 1.4426950408889634


def shifted(value, axis, steps):
    count = lax.axis_size(axis)
    pairs = [(source, (source + steps) % count) for source in range(count)]
    return lax.ppermute(value, axis, pairs)


def exchanged(value):
    return lax.all_to_all(value, "inner", split_axis=0, concat_axis=0, tiled=True)


def dot(a, b):
    return lax.dot_general(a, b, (((1,), (0,)), ((), ())), preferred_element_type=jnp.float32)


def dot_t(a, b):
    return lax.dot_general(a, b, (((1,), (1,)), ((), ())), preferred_element_type=jnp.float32)


def pack_kernel(a_ref, b_ref, o_ref):
    peers, heads = o_ref.shape[0], o_ref.shape[1]
    for peer in range(peers):
        for head in range(heads):
            at = (peer * heads + head) * HEAD
            o_ref[peer, head, 0] = a_ref[:, at : at + HEAD]
            o_ref[peer, head, 1] = b_ref[:, at : at + HEAD]


def pack(a, b, peers):
    rows, width = a.shape
    heads = width // HEAD // peers
    return pl.pallas_call(
        pack_kernel,
        out_shape=jax.ShapeDtypeStruct((peers, heads, 2, rows, HEAD), a.dtype),
    )(a, b)


def unpack_kernel(i_ref, a_ref, b_ref):
    peers, heads = i_ref.shape[0], i_ref.shape[1]
    for peer in range(peers):
        for head in range(heads):
            at = (peer * heads + head) * HEAD
            a_ref[:, at : at + HEAD] = i_ref[peer, head, 0]
            b_ref[:, at : at + HEAD] = i_ref[peer, head, 1]


def unpack(packed):
    peers, heads, _, rows, _ = packed.shape
    shape = jax.ShapeDtypeStruct((rows, peers * heads * HEAD), packed.dtype)
    return pl.pallas_call(unpack_kernel, out_shape=(shape, shape))(packed)


def attention_kernel(bias_ref, qg_ref, kv0_ref, kv1_ref, oq_ref, own_ref, prev_ref, acc_k, acc_v, s_ref):
    step = pl.program_id(1)
    span = kv0_ref.shape[0] * kv0_ref.shape[3]
    keys = (kv0_ref[:, 0, 0].reshape(span, HEAD), kv1_ref[:, 0, 0].reshape(span, HEAD))
    vals = (kv0_ref[:, 0, 1].reshape(span, HEAD), kv1_ref[:, 0, 1].reshape(span, HEAD))
    q = qg_ref[:, 0, 0].reshape(TILE, HEAD)
    g = qg_ref[:, 0, 1].reshape(TILE, HEAD)

    @pl.when(step == 0)
    def _():
        acc_k[...] = jnp.zeros_like(acc_k)
        acc_v[...] = jnp.zeros_like(acc_v)

    for half in range(2):
        s = dot_t(q, keys[half]) * (SCALE * LOG2E)
        for j in range(TILE // CH):
            rows = slice(j * CH, (j + 1) * CH)
            cols = slice(half * span, (half + 1) * span)
            s_ref[rows, cols] = s[rows] + bias_ref[0, j : j + 1, cols]
    row = lax.broadcasted_iota(jnp.int32, (TILE, TILE), 0)
    col = lax.broadcasted_iota(jnp.int32, (TILE, TILE), 1)
    later = jnp.logical_and(row // CH == col // CH, col > row)
    own = pl.ds(pl.multiple_of(step * TILE, TILE), TILE)
    s_ref[:, own] = s_ref[:, own] + jnp.where(later, NEG, 0.0)

    s = s_ref[...]
    top = jnp.max(s, axis=1, keepdims=True)
    e = jnp.exp2(s - top)
    total = jnp.sum(e, axis=1, keepdims=True)
    p = e * (1.0 / total)
    pb = p.astype(jnp.bfloat16)
    out = (dot(pb[:, :span], vals[0]) + dot(pb[:, span:], vals[1])).astype(jnp.bfloat16)
    delta = jnp.sum(g.astype(jnp.float32) * out.astype(jnp.float32), axis=1, keepdims=True)
    dq = jnp.zeros((TILE, HEAD), jnp.float32)
    qt = q.T
    gt = g.T
    for half in range(2):
        cols = slice(half * span, (half + 1) * span)
        dp = dot_t(g, vals[half])
        ds = (p[:, cols] * (dp - delta)).astype(jnp.bfloat16)
        dq = dq + dot(ds, keys[half])
        acc_k[:, cols] += dot(qt, ds)
        acc_v[:, cols] += dot(gt, pb[:, cols])
    oq_ref[:, 0, 0] = out.reshape(oq_ref.shape[0], -1, HEAD)
    oq_ref[:, 0, 1] = (dq * SCALE).astype(jnp.bfloat16).reshape(oq_ref.shape[0], -1, HEAD)

    @pl.when(step == pl.num_programs(1) - 1)
    def _():
        blocks = own_ref.shape[0]
        rows = own_ref.shape[3]
        for which, acc, factor in ((0, acc_k, SCALE), (1, acc_v, 1.0)):
            for block in range(blocks):
                at = block * rows
                own_ref[block, 0, which] = (acc[:, at : at + rows].T * factor).astype(own_ref.dtype)
                at += span
                prev_ref[block, 0, which] = (acc[:, at : at + rows].T * factor).astype(prev_ref.dtype)


def attention(bias, qg, kv0, kv1):
    peers, heads, _, rows, _ = qg.shape
    tiles = peers * rows // TILE
    per = TILE // rows
    whole = pl.BlockSpec((peers, 1, 2, rows, HEAD), lambda h, i: (0, h, 0, 0, 0))
    tile = pl.BlockSpec((per, 1, 2, rows, HEAD), lambda h, i: (i, h, 0, 0, 0))
    shape = jax.ShapeDtypeStruct(qg.shape, jnp.bfloat16)
    width = 2 * peers * rows
    return pl.pallas_call(
        attention_kernel,
        grid=(heads, tiles),
        in_specs=[
            pl.BlockSpec((1, TILE // CH, width), lambda h, i: (i, 0, 0)),
            tile,
            whole,
            whole,
        ],
        out_specs=(tile, whole, whole),
        out_shape=(shape, jax.ShapeDtypeStruct(qg.shape, jnp.float32), shape),
        scratch_shapes=[
            pltpu.VMEM((HEAD, width), jnp.float32),
            pltpu.VMEM((HEAD, width), jnp.float32),
            pltpu.VMEM((TILE, width), jnp.float32),
        ],
        compiler_params=pltpu.CompilerParams(vmem_limit_bytes=48 * 2**20),
    )(bias, qg, kv0, kv1)


def window_bias(stretch_pos, block_mask, group, groups, span):
    prev = (group + groups - 1) % groups
    own_pos = lax.dynamic_slice_in_dim(stretch_pos, group * span, span, 0)
    prev_pos = lax.dynamic_slice_in_dim(stretch_pos, prev * span, span, 0)
    key_pos = jnp.concatenate([own_pos, prev_pos], axis=0)
    flags = lax.dynamic_slice_in_dim(block_mask, group * span, span, 0)
    seen = jnp.logical_and(flags == 1, key_pos[None, :] <= own_pos[:, None])
    bias = jnp.where(seen, 0.0, NEG).astype(jnp.float32)
    wide = jnp.broadcast_to(bias[:, :, None], bias.shape + (CH,))
    return wide.reshape(span * CH // TILE, TILE // CH, -1)


def body(queries, keys, values, out_grad, stretch_pos, block_mask):
    peers = lax.axis_size("inner")
    groups = lax.axis_size("outer")
    group = lax.axis_index("outer")
    bias = window_bias(stretch_pos, block_mask, group, groups, 2 * peers)
    kv = exchanged(pack(keys, values, peers))
    prev_kv = shifted(kv, "outer", 1)
    qg = exchanged(pack(queries, out_grad, peers))
    oq, own, prev = attention(bias, qg, kv, prev_kv)
    back = shifted(prev, "outer", -1)
    output, dquery = unpack(exchanged(oq))
    dkv = (own + back.astype(jnp.float32)).astype(jnp.bfloat16)
    d_key, d_value = unpack(exchanged(dkv))
    return (output, dquery, d_key, d_value)


def solution(mesh):
    rows = P(("outer", "inner"), None)
    return jax.shard_map(
        body,
        mesh=mesh,
        in_specs=(rows, rows, rows, rows, P(), P()),
        out_specs=(rows, rows, rows, rows),
        check_vma=False,
    )
```

```python
import jax
import jax.numpy as jnp
from jax import lax
from jax.experimental import pallas as pl
from jax.experimental.pallas import tpu as pltpu
from jax.sharding import PartitionSpec as P

H = 16
HEAD = 128
CH = 64
NEG = -1e30
TILE = 256
SCALE = 1.0 / HEAD**0.5
LOG2E = 1.4426950408889634
RUN = 8


def exchanged(value):
    return lax.all_to_all(value, "inner", split_axis=0, concat_axis=0, tiled=True)


def added(a, b):
    return (a.astype(jnp.float32) + b.astype(jnp.float32)).astype(jnp.bfloat16)


def dot(a, b):
    return lax.dot_general(a, b, (((1,), (0,)), ((), ())), preferred_element_type=jnp.float32)


def dot_t(a, b):
    return lax.dot_general(a, b, (((1,), (1,)), ((), ())), preferred_element_type=jnp.float32)


def pack_kernel(a_ref, b_ref, o_ref):
    peers, heads = o_ref.shape[0], o_ref.shape[1]
    for peer in range(peers):
        for head in range(heads):
            at = (peer * heads + head) * HEAD
            o_ref[peer, head, 0] = a_ref[:, at : at + HEAD]
            o_ref[peer, head, 1] = b_ref[:, at : at + HEAD]


def pack(a, b, peers):
    rows, width = a.shape
    heads = width // HEAD // peers
    return pl.pallas_call(
        pack_kernel,
        out_shape=jax.ShapeDtypeStruct((peers, heads, 2, rows, HEAD), a.dtype),
    )(a, b)


def unpack_kernel(*refs):
    parts, (a_ref, b_ref) = refs[:-2], refs[-2:]
    heads = len(parts)
    for head, part in enumerate(parts):
        for peer in range(part.shape[0]):
            at = (peer * heads + head) * HEAD
            a_ref[:, at : at + HEAD] = part[peer, 0]
            b_ref[:, at : at + HEAD] = part[peer, 1]


def unpack(parts):
    peers, _, rows, _ = parts[0].shape
    shape = jax.ShapeDtypeStruct((rows, peers * len(parts) * HEAD), parts[0].dtype)
    return pl.pallas_call(unpack_kernel, out_shape=(shape, shape))(*parts)


def split_kernel(i_ref, a_ref, b_ref):
    peers, heads = i_ref.shape[0], i_ref.shape[1]
    for peer in range(peers):
        for head in range(heads):
            at = (peer * heads + head) * HEAD
            a_ref[:, at : at + HEAD] = i_ref[peer, head, 0]
            b_ref[:, at : at + HEAD] = i_ref[peer, head, 1]


def split(packed):
    peers, heads, _, rows, _ = packed.shape
    shape = jax.ShapeDtypeStruct((rows, peers * heads * HEAD), packed.dtype)
    return pl.pallas_call(split_kernel, out_shape=(shape, shape))(packed)


def attention_kernel(bias_ref, qg_ref, kv0_ref, kv1_ref, oq_ref, own_ref, prev_ref, acc_k, acc_v, s_ref):
    step = pl.program_id(0)
    span = kv1_ref.shape[0] * kv1_ref.shape[2]
    keys = (kv0_ref[:, 0, 0].reshape(span, HEAD), kv1_ref[:, 0].reshape(span, HEAD))
    vals = (kv0_ref[:, 0, 1].reshape(span, HEAD), kv1_ref[:, 1].reshape(span, HEAD))
    q = qg_ref[:, 0, 0].reshape(TILE, HEAD)
    g = qg_ref[:, 0, 1].reshape(TILE, HEAD)

    @pl.when(step == 0)
    def _():
        acc_k[...] = jnp.zeros_like(acc_k)
        acc_v[...] = jnp.zeros_like(acc_v)

    for half in range(2):
        s = dot_t(q, keys[half]) * (SCALE * LOG2E)
        for j in range(TILE // CH):
            rows = slice(j * CH, (j + 1) * CH)
            cols = slice(half * span, (half + 1) * span)
            s_ref[rows, cols] = s[rows] + bias_ref[0, j : j + 1, cols]
    row = lax.broadcasted_iota(jnp.int32, (TILE, TILE), 0)
    col = lax.broadcasted_iota(jnp.int32, (TILE, TILE), 1)
    later = jnp.logical_and(row // CH == col // CH, col > row)
    own = pl.ds(pl.multiple_of(step * TILE, TILE), TILE)
    s_ref[:, own] = s_ref[:, own] + jnp.where(later, NEG, 0.0)

    s = s_ref[...]
    top = jnp.max(s, axis=1, keepdims=True)
    e = jnp.exp2(s - top)
    total = jnp.sum(e, axis=1, keepdims=True)
    p = e * (1.0 / total)
    pb = p.astype(jnp.bfloat16)
    out = (dot(pb[:, :span], vals[0]) + dot(pb[:, span:], vals[1])).astype(jnp.bfloat16)
    delta = jnp.sum(g.astype(jnp.float32) * out.astype(jnp.float32), axis=1, keepdims=True)
    dq = jnp.zeros((TILE, HEAD), jnp.float32)
    qt = q.T
    gt = g.T
    for half in range(2):
        cols = slice(half * span, (half + 1) * span)
        dp = dot_t(g, vals[half])
        ds = (p[:, cols] * (dp - delta)).astype(jnp.bfloat16)
        dq = dq + dot(ds, keys[half])
        acc_k[:, cols] += dot(qt, ds)
        acc_v[:, cols] += dot(gt, pb[:, cols])
    oq_ref[:, 0] = out.reshape(oq_ref.shape[0], -1, HEAD)
    oq_ref[:, 1] = (dq * SCALE).astype(jnp.bfloat16).reshape(oq_ref.shape[0], -1, HEAD)

    @pl.when(step == pl.num_programs(0) - 1)
    def _():
        blocks = own_ref.shape[0]
        rows = own_ref.shape[2]
        for which, acc, factor in ((0, acc_k, SCALE), (1, acc_v, 1.0)):
            for block in range(blocks):
                at = block * rows
                own_ref[block, which] = (acc[:, at : at + rows].T * factor).astype(own_ref.dtype)
                at += span
                prev_ref[block, which] = (acc[:, at : at + rows].T * factor).astype(prev_ref.dtype)


def attention(bias, qg, kv0, kv1, head):
    peers, _, _, rows, _ = qg.shape
    tiles = peers * rows // TILE
    per = TILE // rows
    width = 2 * peers * rows
    whole = pl.BlockSpec((peers, 2, rows, HEAD), lambda i: (0, 0, 0, 0))
    shape = jax.ShapeDtypeStruct((peers, 2, rows, HEAD), jnp.bfloat16)
    return pl.pallas_call(
        attention_kernel,
        grid=(tiles,),
        in_specs=[
            pl.BlockSpec((1, TILE // CH, width), lambda i: (i, 0, 0)),
            pl.BlockSpec((per, 1, 2, rows, HEAD), lambda i: (i, head, 0, 0, 0)),
            pl.BlockSpec((peers, 1, 2, rows, HEAD), lambda i: (0, head, 0, 0, 0)),
            whole,
        ],
        out_specs=(pl.BlockSpec((per, 2, rows, HEAD), lambda i: (i, 0, 0, 0)), whole, whole),
        out_shape=(pltpu.HBM(shape.shape, shape.dtype), shape, shape),
        scratch_shapes=[
            pltpu.VMEM((HEAD, width), jnp.float32),
            pltpu.VMEM((HEAD, width), jnp.float32),
            pltpu.VMEM((TILE, width), jnp.float32),
        ],
        compiler_params=pltpu.CompilerParams(vmem_limit_bytes=48 * 2**20),
        cost_estimate=pl.CostEstimate(flops=12 * 10**9, bytes_accessed=4 * 2**20, transcendentals=2 * 2**20),
    )(bias, qg, kv0, kv1)


def window_bias(stretch_pos, block_mask, group, groups, span):
    prev = (group + groups - 1) % groups
    own_pos = lax.dynamic_slice_in_dim(stretch_pos, group * span, span, 0)
    prev_pos = lax.dynamic_slice_in_dim(stretch_pos, prev * span, span, 0)
    key_pos = jnp.concatenate([own_pos, prev_pos], axis=0)
    flags = lax.dynamic_slice_in_dim(block_mask, group * span, span, 0)
    seen = jnp.logical_and(flags == 1, key_pos[None, :] <= own_pos[:, None])
    bias = jnp.where(seen, 0.0, NEG).astype(jnp.float32)
    wide = jnp.broadcast_to(bias[:, :, None], bias.shape + (CH,))
    return wide.reshape(span * CH // TILE, TILE // CH, -1)


def hop(value, pairs, count):
    flat = [(i * count + s, j * count + d) for (s, i), (d, j) in pairs]
    return lax.ppermute(value, ("inner", "outer"), flat)


def shifted(value, steps, relay):
    count, peers = lax.axis_size("outer"), lax.axis_size("inner")
    edge, entry = (RUN - 1, 0) if steps == 1 else (0, RUN - 1)
    first, second = [], []
    for s in range(count):
        for i in range(peers):
            to = (s + steps) % count
            if s % RUN == edge and i in relay:
                near = s // RUN * RUN + entry
                first.append(((s, i), (near, i)))
                second.append(((near, i), (to, i)))
            else:
                first.append(((s, i), (to, i)))
    got = hop(value, first, count)
    if not second:
        return got
    far = hop(got, second, count)
    inner = lax.axis_index("inner")
    relayed = jnp.logical_and(lax.axis_index("outer") % RUN == entry, jnp.logical_and(inner >= relay[0], inner <= relay[-1]))
    return jnp.where(relayed, far, got)


def body(queries, keys, values, out_grad, stretch_pos, block_mask):
    peers = lax.axis_size("inner")
    groups = lax.axis_size("outer")
    group = lax.axis_index("outer")
    bias = window_bias(stretch_pos, block_mask, group, groups, 2 * peers)
    kv = exchanged(pack(keys, values, peers))
    head0, head1, packed = lax.optimization_barrier((kv[:, 0], kv[:, 1], pack(queries, out_grad, peers)))
    prev_kv0 = shifted(head0, 1, range(peers))
    prev_kv1 = shifted(head1, 1, ())
    qg = exchanged(packed)
    oq0, own0, prev0 = attention(bias, qg, kv, prev_kv0, 0)
    own0, bias = lax.optimization_barrier((own0, bias))
    oq0 = exchanged(oq0)
    back0 = shifted(prev0, -1, ())
    oq1, own1, prev1 = attention(bias, qg, kv, prev_kv1, 1)
    oq0, oq1 = lax.optimization_barrier((oq0, oq1))
    back0, prev1 = lax.optimization_barrier((back0, prev1))
    back1 = shifted(prev1, -1, range(peers // 2, peers))
    oq1 = exchanged(oq1)
    output, dquery = unpack([oq0, oq1])
    own = jnp.stack([own0, own1], axis=1)
    back = jnp.stack([back0, back1], axis=1)
    d_key, d_value = split(exchanged(added(own, back)))
    return (output, dquery, d_key, d_value)


def solution(mesh):
    rows = P(("outer", "inner"), None)
    return jax.shard_map(
        body,
        mesh=mesh,
        in_specs=(rows, rows, rows, rows, P(), P()),
        out_specs=(rows, rows, rows, rows),
        check_vma=False,
    )
```

```python
import jax
import jax.numpy as jnp
from jax import lax
from jax.experimental import pallas as pl
from jax.experimental.pallas import tpu as pltpu
from jax.sharding import PartitionSpec as P

H = 16
HEAD = 128
CH = 64
NEG = -1e30
TILE = 256
SCALE = 1.0 / HEAD**0.5
LOG2E = 1.4426950408889634
RUN = 8


def exchanged(value):
    return lax.all_to_all(value, "inner", split_axis=0, concat_axis=0, tiled=True)


def added(a, b):
    return (a.astype(jnp.float32) + b.astype(jnp.float32)).astype(jnp.bfloat16)


def dot(a, b):
    return lax.dot_general(a, b, (((1,), (0,)), ((), ())), preferred_element_type=jnp.float32)


def dot_t(a, b):
    return lax.dot_general(a, b, (((1,), (1,)), ((), ())), preferred_element_type=jnp.float32)


def pack_kernel(a_ref, b_ref, *o_refs):
    for peer in range(o_refs[0].shape[0]):
        for head, o_ref in enumerate(o_refs):
            at = (peer * len(o_refs) + head) * HEAD
            for which, ref in enumerate((a_ref, b_ref)):
                o_ref[peer, which] = ref[:, at : at + HEAD]


def pack(a, b, peers):
    rows, width = a.shape
    shape = pltpu.HBM((peers, 2, rows, HEAD), a.dtype)
    return pl.pallas_call(pack_kernel, out_shape=(shape,) * (width // HEAD // peers))(a, b)


def unpack_kernel(i_ref, a_ref, b_ref, va, vb, come, go):
    peers, heads = i_ref.shape[:2]
    held = []
    for which, to in enumerate((va, vb)):
        for at in range(peers * heads):
            part = i_ref.at[at // heads, at % heads, which]
            held.append(pltpu.make_async_copy(part, to.at[:, pl.ds(at * HEAD, HEAD)], come.at[at, which]))
            held[-1].start()
    for copy in held:
        copy.wait()
    held = [pltpu.make_async_copy(x, y, go.at[n]) for n, (x, y) in enumerate(((va, a_ref), (vb, b_ref)))]
    for copy in held:
        copy.start()
    for copy in held:
        copy.wait()


def unpack(packed):
    peers, heads, _, rows, _ = packed.shape
    shape = pltpu.HBM((rows, peers * heads * HEAD), packed.dtype)
    room = pltpu.VMEM((rows, peers * heads * HEAD), packed.dtype)
    return pl.pallas_call(
        unpack_kernel,
        out_shape=(shape, shape),
        in_specs=[pl.BlockSpec(memory_space=pl.ANY)],
        out_specs=(pl.BlockSpec(memory_space=pltpu.HBM),) * 2,
        scratch_shapes=[room, room, pltpu.SemaphoreType.DMA((peers * heads, 2)), pltpu.SemaphoreType.DMA((2,))],
        compiler_params=pltpu.CompilerParams(vmem_limit_bytes=48 * 2**20),
    )(packed)


def attend(bias_ref, qg_ref, keys, vals, put, acc_k, acc_v, s_ref, dp_ref):
    span = keys[0].shape[0]
    rows = qg_ref.shape[2]
    per = TILE // rows
    row = lax.broadcasted_iota(jnp.int32, (TILE, TILE), 0)
    col = lax.broadcasted_iota(jnp.int32, (TILE, TILE), 1)
    later = jnp.where(jnp.logical_and(row // CH == col // CH, col > row), NEG, 0.0)
    halves = [slice(half * span, (half + 1) * span) for half in range(2)]

    def scores(tile):
        q = qg_ref[tile * per : (tile + 1) * per, 0].reshape(TILE, HEAD)
        g = qg_ref[tile * per : (tile + 1) * per, 1].reshape(TILE, HEAD)
        own = slice(tile * TILE, (tile + 1) * TILE)
        for half, cols in enumerate(halves):
            seen = [bias_ref[0, at // CH : at // CH + 1, cols] for at in range(own.start, own.stop, CH)]
            seen = jnp.concatenate([jnp.broadcast_to(line, (CH, span)) for line in seen], axis=0)
            s = dot_t(q, keys[half]) * (SCALE * LOG2E) + seen
            if half == 0:
                parts = (s[:, : own.start], s[:, own] + later, s[:, own.stop :])
                s = jnp.concatenate([part for part in parts if part.shape[1]], axis=1)
            s_ref[tile % 2, :, cols] = s
            dp_ref[tile % 2, :, cols] = dot_t(g, vals[half])
        return q, g

    def finish(tile, q, g):
        s = s_ref[tile % 2]
        top = jnp.max(s, axis=1, keepdims=True)
        e = jnp.exp2(s - top)
        total = jnp.sum(e, axis=1, keepdims=True)
        p = e * (1.0 / total)
        pb = p.astype(jnp.bfloat16)
        out = (dot(pb[:, halves[0]], vals[0]) + dot(pb[:, halves[1]], vals[1])).astype(jnp.bfloat16)
        delta = jnp.sum(g.astype(jnp.float32) * out.astype(jnp.float32), axis=1, keepdims=True)
        dq = jnp.zeros((TILE, HEAD), jnp.float32)
        qt, gt = q.T, g.T
        for half, cols in enumerate(halves):
            ds = (p[:, cols] * (dp_ref[tile % 2, :, cols] - delta)).astype(jnp.bfloat16)
            dq = dq + dot(ds, keys[half])
            for acc, term in ((acc_k, dot(qt, ds)), (acc_v, dot(gt, pb[:, cols]))):
                acc[:, cols] = term if tile == 0 else acc[:, cols] + term
        put(slice(tile * per, (tile + 1) * per), out, (dq * SCALE).astype(jnp.bfloat16))

    tiles = span // TILE
    after = scores(0)
    for tile in range(tiles):
        now = after
        if tile + 1 < tiles:
            after = scores(tile + 1)
        finish(tile, *now)


def attention_kernel(bias_ref, qg_ref, own_ref, prev_ref, *rest):
    oq_ref, d_ref, back_ref = rest[-7:-4]
    scratch = rest[-4:]
    peers, _, rows, _ = own_ref.shape

    def put(blocks, out, dq):
        for which, value in ((0, out), (1, dq)):
            oq_ref[blocks, 0, which] = value.reshape(-1, rows, HEAD)

    keys, vals = ((own_ref[:, w].reshape(-1, HEAD), prev_ref[:, w].reshape(-1, HEAD)) for w in range(2))
    attend(bias_ref, qg_ref, keys, vals, put, *scratch)
    for which, acc, factor in ((0, scratch[0], SCALE), (1, scratch[1], 1.0)):
        for block in range(peers):
            at = block * rows
            d_ref[block, 0, which] = (acc[:, at : at + rows].T * factor).astype(d_ref.dtype)
            at += peers * rows
            back_ref[block, which] = (acc[:, at : at + rows].T * factor).astype(back_ref.dtype)


def attention(bias, qg, own, prev, head, heads, *held):
    peers, _, rows, _ = own.shape
    width = 2 * peers * rows
    whole = pl.BlockSpec(own.shape, lambda i: (0, 0, 0, 0))
    slot = pl.BlockSpec((peers, 1, 2, rows, HEAD), lambda i: (0, head, 0, 0, 0))
    both = pltpu.HBM((peers, heads, 2, rows, HEAD), own.dtype)
    return pl.pallas_call(
        attention_kernel,
        grid=(1,),
        in_specs=[pl.BlockSpec((1, width // 2 // CH, width), lambda i: (0, 0, 0)), whole, whole, whole]
        + [pl.BlockSpec(memory_space=pl.ANY)] * len(held),
        out_specs=(slot, slot, whole),
        out_shape=(both, both, jax.ShapeDtypeStruct(own.shape, own.dtype)),
        input_output_aliases={4 + n: n for n in range(len(held))},
        scratch_shapes=[pltpu.VMEM((HEAD, width), jnp.float32)] * 2 + [pltpu.VMEM((2, TILE, width), jnp.float32)] * 2,
        compiler_params=pltpu.CompilerParams(vmem_limit_bytes=48 * 2**20),
        cost_estimate=pl.CostEstimate(flops=12 * 10**9, bytes_accessed=4 * 2**20, transcendentals=2 * 2**20),
    )(bias, qg, own, prev, *held)


def window_bias(stretch_pos, block_mask, group, groups, span):
    prev = (group + groups - 1) % groups
    own_pos = lax.dynamic_slice_in_dim(stretch_pos, group * span, span, 0)
    prev_pos = lax.dynamic_slice_in_dim(stretch_pos, prev * span, span, 0)
    key_pos = jnp.concatenate([own_pos, prev_pos], axis=0)
    flags = lax.dynamic_slice_in_dim(block_mask, group * span, span, 0)
    seen = jnp.logical_and(flags == 1, key_pos[None, :] <= own_pos[:, None])
    bias = jnp.where(seen, 0.0, NEG).astype(jnp.float32)
    wide = jnp.broadcast_to(bias[:, :, None], bias.shape + (CH,))
    return wide.reshape(1, span, -1)


def hop(value, pairs, count):
    flat = [(i * count + s, j * count + d) for (s, i), (d, j) in pairs]
    return lax.ppermute(value, ("inner", "outer"), flat)


def routes(steps, relay, count, peers):
    edge, entry = (RUN - 1, 0) if steps == 1 else (0, RUN - 1)
    within, direct, second = [], [], []
    for s in range(count):
        for i in range(peers):
            to = (s + steps) % count
            if s % RUN != edge:
                within.append(((s, i), (to, i)))
            elif i in relay:
                near = s // RUN * RUN + entry
                within.append(((s, i), (near, i)))
                second.append(((near, i), (to, i)))
            else:
                direct.append(((s, i), (to, i)))
    return within, direct, second


def sent(value, steps, relay):
    count, peers = lax.axis_size("outer"), lax.axis_size("inner")
    within, direct, second = routes(steps, relay, count, peers)
    across = hop(value, direct, count) if direct else None

    def finish(near):
        far = hop(near, second, count) if second else across
        if direct and second:
            inner = lax.axis_index("inner")
            far = jnp.where(jnp.logical_and(inner >= relay[0], inner <= relay[-1]), far, across)
        return jnp.where(lax.axis_index("outer") % RUN == (0 if steps == 1 else RUN - 1), far, near)

    return hop(value, within, count), finish


def shifted(value, steps):
    count = lax.axis_size("outer")
    return lax.ppermute(value, "outer", [(s, (s + steps) % count) for s in range(count)])


def after(value, *earlier):
    return lax.optimization_barrier((value, *earlier))


def add_at(d, head, back):
    own = lax.index_in_dim(d, head, 1, keepdims=False)
    return lax.dynamic_update_slice_in_dim(d, added(own, back)[:, None], head, axis=1)


def body(queries, keys, values, out_grad, stretch_pos, block_mask):
    peers = lax.axis_size("inner")
    groups = lax.axis_size("outer")
    bias = window_bias(stretch_pos, block_mask, lax.axis_index("outer"), groups, 2 * peers)
    upper = range(peers // 2, peers)
    kv0, kv1 = pack(keys, values, peers)
    qg0, qg1 = pack(queries, out_grad, peers)
    kv0 = exchanged(kv0)
    kv1, kv0 = after(kv1, kv0)
    near, finish = sent(kv0, 1, upper)
    kv1 = exchanged(kv1)
    qg0, kv1, near = after(qg0, kv1, near)
    prev_kv1 = shifted(kv1, 1)
    qg0 = exchanged(qg0)
    prev_kv0 = finish(near)
    qg1, qg0 = after(qg1, qg0)
    qg1 = exchanged(qg1)
    oq, d, back0 = attention(bias, qg0, kv0, prev_kv0, 0, 2)
    back0 = shifted(back0, -1)
    oq, d, back1 = attention(bias, qg1, kv1, prev_kv1, 1, 2, oq, d)
    back1, back0 = after(back1, back0)
    near, finish = sent(back1, -1, upper)
    oq = exchanged(oq)
    d = add_at(d, 0, back0)
    d = add_at(d, 1, finish(near))
    d, oq = after(d, oq)
    output, dquery = unpack(oq)
    d_key, d_value = unpack(exchanged(d))
    return (output, dquery, d_key, d_value)


def solution(mesh):
    rows = P(("outer", "inner"), None)
    return jax.shard_map(
        body,
        mesh=mesh,
        in_specs=(rows, rows, rows, rows, P(), P()),
        out_specs=(rows, rows, rows, rows),
        check_vma=False,
    )
```

```python
import jax
import jax.numpy as jnp
from jax import lax
from jax.experimental import pallas as pl
from jax.experimental.pallas import tpu as pltpu
from jax.sharding import PartitionSpec as P

H = 16
HEAD = 128
CH = 64
NEG = -1e30
TILE = 256
SCALE = 1.0 / HEAD**0.5
LOG2E = 1.4426950408889634
RUN = 8


def exchanged(value):
    return lax.all_to_all(value, "inner", split_axis=0, concat_axis=0, tiled=True)


def added(a, b):
    return (a.astype(jnp.float32) + b.astype(jnp.float32)).astype(jnp.bfloat16)


def dot(a, b):
    return lax.dot_general(a, b, (((1,), (0,)), ((), ())), preferred_element_type=jnp.float32)


def dot_t(a, b):
    return lax.dot_general(a, b, (((1,), (1,)), ((), ())), preferred_element_type=jnp.float32)


def pack_kernel(a_ref, b_ref, o_ref):
    peers, heads = o_ref.shape[:2]
    for at in range(peers * heads):
        for which, ref in enumerate((a_ref, b_ref)):
            o_ref[at // heads, at % heads, which] = ref[:, at * HEAD : (at + 1) * HEAD]


def pack(a, b, peers):
    rows, width = a.shape
    shape = pltpu.HBM((peers, width // HEAD // peers, 2, rows, HEAD), a.dtype)
    return pl.pallas_call(pack_kernel, out_shape=shape)(a, b)


def unpack_kernel(i_ref, a_ref, b_ref, va, vb, come, go):
    peers, heads = i_ref.shape[:2]
    held = []
    for which, to in enumerate((va, vb)):
        for at in range(peers * heads):
            part = i_ref.at[at // heads, at % heads, which]
            held.append(pltpu.make_async_copy(part, to.at[:, pl.ds(at * HEAD, HEAD)], come.at[at, which]))
            held[-1].start()
    for copy in held:
        copy.wait()
    held = [pltpu.make_async_copy(x, y, go.at[n]) for n, (x, y) in enumerate(((va, a_ref), (vb, b_ref)))]
    for copy in held:
        copy.start()
    for copy in held:
        copy.wait()


def unpack(packed):
    peers, heads, _, rows, _ = packed.shape
    shape = pltpu.HBM((rows, peers * heads * HEAD), packed.dtype)
    room = pltpu.VMEM((rows, peers * heads * HEAD), packed.dtype)
    return pl.pallas_call(
        unpack_kernel,
        out_shape=(shape, shape),
        in_specs=[pl.BlockSpec(memory_space=pl.ANY)],
        out_specs=(pl.BlockSpec(memory_space=pltpu.HBM),) * 2,
        scratch_shapes=[room, room, pltpu.SemaphoreType.DMA((peers * heads, 2)), pltpu.SemaphoreType.DMA((2,))],
        compiler_params=pltpu.CompilerParams(vmem_limit_bytes=48 * 2**20),
    )(packed)


def attend(bias_ref, qg_ref, keys, vals, put, acc_k, acc_v, s_ref, dp_ref):
    span = keys[0].shape[0]
    rows = qg_ref.shape[3]
    per = TILE // rows
    row = lax.broadcasted_iota(jnp.int32, (TILE, TILE), 0)
    col = lax.broadcasted_iota(jnp.int32, (TILE, TILE), 1)
    later = jnp.where(jnp.logical_and(row // CH == col // CH, col > row), NEG, 0.0)
    halves = [slice(half * span, (half + 1) * span) for half in range(2)]

    def scores(tile):
        q = qg_ref[tile * per : (tile + 1) * per, 0, 0].reshape(TILE, HEAD)
        g = qg_ref[tile * per : (tile + 1) * per, 0, 1].reshape(TILE, HEAD)
        own = slice(tile * TILE, (tile + 1) * TILE)
        for half, cols in enumerate(halves):
            seen = [bias_ref[0, at // CH : at // CH + 1, cols] for at in range(own.start, own.stop, CH)]
            seen = jnp.concatenate([jnp.broadcast_to(line, (CH, span)) for line in seen], axis=0)
            s = dot_t(q, keys[half]) * (SCALE * LOG2E) + seen
            if half == 0:
                parts = (s[:, : own.start], s[:, own] + later, s[:, own.stop :])
                s = jnp.concatenate([part for part in parts if part.shape[1]], axis=1)
            s_ref[tile % 2, :, cols] = s
            dp_ref[tile % 2, :, cols] = dot_t(g, vals[half])
        return q, g

    def finish(tile, q, g):
        s = s_ref[tile % 2]
        top = jnp.max(s, axis=1, keepdims=True)
        e = jnp.exp2(s - top)
        total = jnp.sum(e, axis=1, keepdims=True)
        p = e * (1.0 / total)
        pb = p.astype(jnp.bfloat16)
        out = (dot(pb[:, halves[0]], vals[0]) + dot(pb[:, halves[1]], vals[1])).astype(jnp.bfloat16)
        delta = jnp.sum(g.astype(jnp.float32) * out.astype(jnp.float32), axis=1, keepdims=True)
        dq = jnp.zeros((TILE, HEAD), jnp.float32)
        qt, gt = q.T, g.T
        for half, cols in enumerate(halves):
            ds = (p[:, cols] * (dp_ref[tile % 2, :, cols] - delta)).astype(jnp.bfloat16)
            dq = dq + dot(ds, keys[half])
            for acc, term in ((acc_k, dot(qt, ds)), (acc_v, dot(gt, pb[:, cols]))):
                acc[:, cols] = term if tile == 0 else acc[:, cols] + term
        put(slice(tile * per, (tile + 1) * per), out, (dq * SCALE).astype(jnp.bfloat16))

    tiles = span // TILE
    after = scores(0)
    for tile in range(tiles):
        now = after
        if tile + 1 < tiles:
            after = scores(tile + 1)
        finish(tile, *now)


def attention_kernel(bias_ref, qg_ref, own_ref, prev_ref, *rest):
    oq_ref, d_ref, back_ref = rest[-7:-4]
    scratch = rest[-4:]
    peers, _, rows, _ = prev_ref.shape

    def put(blocks, out, dq):
        for which, value in ((0, out), (1, dq)):
            oq_ref[blocks, 0, which] = value.reshape(-1, rows, HEAD)

    keys, vals = ((own_ref[:, 0, w].reshape(-1, HEAD), prev_ref[:, w].reshape(-1, HEAD)) for w in range(2))
    attend(bias_ref, qg_ref, keys, vals, put, *scratch)
    for which, acc, factor in ((0, scratch[0], SCALE), (1, scratch[1], 1.0)):
        for block in range(peers):
            at = block * rows
            d_ref[block, 0, which] = (acc[:, at : at + rows].T * factor).astype(d_ref.dtype)
            at += peers * rows
            back_ref[block, which] = (acc[:, at : at + rows].T * factor).astype(back_ref.dtype)


def attention(bias, qg, own, prev, head, *held):
    peers, _, _, rows, _ = own.shape
    width = 2 * peers * rows
    whole = pl.BlockSpec(prev.shape, lambda i: (0, 0, 0, 0))
    slot = pl.BlockSpec((peers, 1, 2, rows, HEAD), lambda i: (0, head, 0, 0, 0))
    both = pltpu.HBM(own.shape, own.dtype)
    return pl.pallas_call(
        attention_kernel,
        grid=(1,),
        in_specs=[pl.BlockSpec((1, width // 2 // CH, width), lambda i: (0, 0, 0)), slot, slot, whole]
        + [pl.BlockSpec(memory_space=pl.ANY)] * len(held),
        out_specs=(slot, slot, whole),
        out_shape=(both, both, jax.ShapeDtypeStruct(prev.shape, prev.dtype)),
        input_output_aliases={4 + n: n for n in range(len(held))},
        scratch_shapes=[pltpu.VMEM((HEAD, width), jnp.float32)] * 2 + [pltpu.VMEM((2, TILE, width), jnp.float32)] * 2,
        compiler_params=pltpu.CompilerParams(vmem_limit_bytes=48 * 2**20),
        cost_estimate=pl.CostEstimate(flops=12 * 10**9, bytes_accessed=4 * 2**20, transcendentals=2 * 2**20),
    )(bias, qg, own, prev, *held)


def window_bias(stretch_pos, block_mask, group, groups, span):
    prev = (group + groups - 1) % groups
    own_pos = lax.dynamic_slice_in_dim(stretch_pos, group * span, span, 0)
    prev_pos = lax.dynamic_slice_in_dim(stretch_pos, prev * span, span, 0)
    key_pos = jnp.concatenate([own_pos, prev_pos], axis=0)
    flags = lax.dynamic_slice_in_dim(block_mask, group * span, span, 0)
    seen = jnp.logical_and(flags == 1, key_pos[None, :] <= own_pos[:, None])
    bias = jnp.where(seen, 0.0, NEG).astype(jnp.float32)
    wide = jnp.broadcast_to(bias[:, :, None], bias.shape + (CH,))
    return wide.reshape(1, span, -1)


def hop(value, pairs, count):
    flat = [(i * count + s, j * count + d) for (s, i), (d, j) in pairs]
    return lax.ppermute(value, ("inner", "outer"), flat)


def routes(steps, relay, count, peers):
    edge, entry = (RUN - 1, 0) if steps == 1 else (0, RUN - 1)
    within, direct, second = [], [], []
    for s in range(count):
        for i in range(peers):
            to = (s + steps) % count
            if s % RUN != edge:
                within.append(((s, i), (to, i)))
            elif i in relay:
                near = s // RUN * RUN + entry
                within.append(((s, i), (near, i)))
                second.append(((near, i), (to, i)))
            else:
                direct.append(((s, i), (to, i)))
    return within, direct, second


def sent(value, steps, relay):
    count, peers = lax.axis_size("outer"), lax.axis_size("inner")
    within, direct, second = routes(steps, relay, count, peers)
    across = hop(value, direct, count) if direct else None

    def finish(near):
        far = hop(near, second, count) if second else across
        if direct and second:
            inner = lax.axis_index("inner")
            far = jnp.where(jnp.logical_and(inner >= relay[0], inner <= relay[-1]), far, across)
        return jnp.where(lax.axis_index("outer") % RUN == (0 if steps == 1 else RUN - 1), far, near)

    return hop(value, within, count), finish


def shifted(value, steps):
    count = lax.axis_size("outer")
    return lax.ppermute(value, "outer", [(s, (s + steps) % count) for s in range(count)])


def after(value, *earlier):
    return lax.optimization_barrier((value, *earlier))


def add_at(d, head, back):
    own = lax.index_in_dim(d, head, 1, keepdims=False)
    return lax.dynamic_update_slice_in_dim(d, added(own, back)[:, None], head, axis=1)


def body(queries, keys, values, out_grad, stretch_pos, block_mask):
    peers = lax.axis_size("inner")
    groups = lax.axis_size("outer")
    bias = window_bias(stretch_pos, block_mask, lax.axis_index("outer"), groups, 2 * peers)
    upper = range(peers // 2, peers)
    kv = exchanged(pack(keys, values, peers))
    kv0, kv1, qg = lax.optimization_barrier((kv[:, 0], kv[:, 1], pack(queries, out_grad, peers)))
    near, finish = sent(kv0, 1, upper)
    prev_kv1 = shifted(kv1, 1)
    qg = exchanged(qg)
    prev_kv0 = finish(near)
    oq, d, back0 = attention(bias, qg, kv, prev_kv0, 0)
    back0 = shifted(back0, -1)
    oq, d, back1 = attention(bias, qg, kv, prev_kv1, 1, oq, d)
    back1, back0 = after(back1, back0)
    near, finish = sent(back1, -1, upper)
    oq = exchanged(oq)
    d = add_at(d, 0, back0)
    d = add_at(d, 1, finish(near))
    d, oq = after(d, oq)
    output, dquery = unpack(oq)
    d_key, d_value = unpack(exchanged(d))
    return (output, dquery, d_key, d_value)


def solution(mesh):
    rows = P(("outer", "inner"), None)
    return jax.shard_map(
        body,
        mesh=mesh,
        in_specs=(rows, rows, rows, rows, P(), P()),
        out_specs=(rows, rows, rows, rows),
        check_vma=False,
    )
```

```python
import jax
import jax.numpy as jnp
from jax import lax
from jax.experimental import pallas as pl
from jax.experimental.pallas import tpu as pltpu
from jax.sharding import PartitionSpec as P

H = 16
HEAD = 128
CH = 64
NEG = -1e30
TILE = 256
SCALE = 1.0 / HEAD**0.5
LOG2E = 1.4426950408889634
RUN = 8


def exchanged(value):
    return lax.all_to_all(value, "inner", split_axis=0, concat_axis=0, tiled=True)


def added(a, b):
    return (a.astype(jnp.float32) + b.astype(jnp.float32)).astype(jnp.bfloat16)


def dot(a, b):
    return lax.dot_general(a, b, (((1,), (0,)), ((), ())), preferred_element_type=jnp.float32)


def dot_t(a, b):
    return lax.dot_general(a, b, (((1,), (1,)), ((), ())), preferred_element_type=jnp.float32)


def pack_kernel(a_ref, b_ref, o_ref):
    peers, heads = o_ref.shape[:2]
    for at in range(peers * heads):
        for which, ref in enumerate((a_ref, b_ref)):
            o_ref[at // heads, at % heads, which] = ref[:, at * HEAD : (at + 1) * HEAD]


def pack(a, b, peers):
    rows, width = a.shape
    heads = width // HEAD // peers
    part = pl.BlockSpec((rows, width // 2), lambda i: (0, i))
    return pl.pallas_call(
        pack_kernel,
        grid=(2,),
        in_specs=[part, part],
        out_specs=pl.BlockSpec((peers // 2, heads, 2, rows, HEAD), lambda i: (i, 0, 0, 0, 0)),
        out_shape=pltpu.HBM((peers, heads, 2, rows, HEAD), a.dtype),
    )(a, b)


def unpack_kernel(i_ref, a_ref, b_ref, va, vb, come, go):
    peers, heads = i_ref.shape[:2]
    held = []
    for which, to in enumerate((va, vb)):
        for at in range(peers * heads):
            part = i_ref.at[at // heads, at % heads, which]
            held.append(pltpu.make_async_copy(part, to.at[:, pl.ds(at * HEAD, HEAD)], come.at[at, which]))
            held[-1].start()
    for copy in held:
        copy.wait()
    held = [pltpu.make_async_copy(x, y, go.at[n]) for n, (x, y) in enumerate(((va, a_ref), (vb, b_ref)))]
    for copy in held:
        copy.start()
    for copy in held:
        copy.wait()


def unpack(packed):
    peers, heads, _, rows, _ = packed.shape
    shape = pltpu.HBM((rows, peers * heads * HEAD), packed.dtype)
    room = pltpu.VMEM((rows, peers * heads * HEAD), packed.dtype)
    return pl.pallas_call(
        unpack_kernel,
        out_shape=(shape, shape),
        in_specs=[pl.BlockSpec(memory_space=pl.ANY)],
        out_specs=(pl.BlockSpec(memory_space=pltpu.HBM),) * 2,
        scratch_shapes=[room, room, pltpu.SemaphoreType.DMA((peers * heads, 2)), pltpu.SemaphoreType.DMA((2,))],
        compiler_params=pltpu.CompilerParams(vmem_limit_bytes=48 * 2**20),
    )(packed)


def attend(bias_ref, qg_ref, keys, vals, put, acc_k, acc_v, s_ref, dp_ref):
    span = keys[0].shape[0]
    rows = qg_ref.shape[3]
    per = TILE // rows
    row = lax.broadcasted_iota(jnp.int32, (TILE, TILE), 0)
    col = lax.broadcasted_iota(jnp.int32, (TILE, TILE), 1)
    later = jnp.where(jnp.logical_and(row // CH == col // CH, col > row), NEG, 0.0)
    halves = [slice(half * span, (half + 1) * span) for half in range(2)]

    def scores(tile):
        q = qg_ref[tile * per : (tile + 1) * per, 0, 0].reshape(TILE, HEAD)
        g = qg_ref[tile * per : (tile + 1) * per, 0, 1].reshape(TILE, HEAD)
        own = slice(tile * TILE, (tile + 1) * TILE)
        for half, cols in enumerate(halves):
            seen = [bias_ref[0, at // CH : at // CH + 1, cols] for at in range(own.start, own.stop, CH)]
            seen = jnp.concatenate([jnp.broadcast_to(line, (CH, span)) for line in seen], axis=0)
            s = dot_t(q, keys[half]) * (SCALE * LOG2E) + seen
            if half == 0:
                parts = (s[:, : own.start], s[:, own] + later, s[:, own.stop :])
                s = jnp.concatenate([part for part in parts if part.shape[1]], axis=1)
            s_ref[tile % 2, :, cols] = s
            dp_ref[tile % 2, :, cols] = dot_t(g, vals[half])
        return q, g

    def finish(tile, q, g):
        s = s_ref[tile % 2]
        top = jnp.max(s, axis=1, keepdims=True)
        e = jnp.exp2(s - top)
        total = jnp.sum(e, axis=1, keepdims=True)
        p = e * (1.0 / total)
        pb = p.astype(jnp.bfloat16)
        out = (dot(pb[:, halves[0]], vals[0]) + dot(pb[:, halves[1]], vals[1])).astype(jnp.bfloat16)
        delta = jnp.sum(g.astype(jnp.float32) * out.astype(jnp.float32), axis=1, keepdims=True)
        dq = jnp.zeros((TILE, HEAD), jnp.float32)
        qt, gt = q.T, g.T
        for half, cols in enumerate(halves):
            ds = (p[:, cols] * (dp_ref[tile % 2, :, cols] - delta)).astype(jnp.bfloat16)
            dq = dq + dot(ds, keys[half])
            for acc, term in ((acc_k, dot(qt, ds)), (acc_v, dot(gt, pb[:, cols]))):
                acc[:, cols] = term if tile == 0 else acc[:, cols] + term
        put(slice(tile * per, (tile + 1) * per), out, (dq * SCALE).astype(jnp.bfloat16))

    tiles = span // TILE
    after = scores(0)
    for tile in range(tiles):
        now = after
        if tile + 1 < tiles:
            after = scores(tile + 1)
        finish(tile, *now)


def attention_kernel(bias_ref, qg_ref, own_ref, prev_ref, *rest):
    oq_ref, d_ref, back_ref = rest[-7:-4]
    scratch = rest[-4:]
    peers, _, rows, _ = prev_ref.shape

    def put(blocks, out, dq):
        for which, value in ((0, out), (1, dq)):
            oq_ref[blocks, 0, which] = value.reshape(-1, rows, HEAD)

    keys, vals = ((own_ref[:, 0, w].reshape(-1, HEAD), prev_ref[:, w].reshape(-1, HEAD)) for w in range(2))
    attend(bias_ref, qg_ref, keys, vals, put, *scratch)
    for which, acc, factor in ((0, scratch[0], SCALE), (1, scratch[1], 1.0)):
        for block in range(peers):
            at = block * rows
            d_ref[block, 0, which] = (acc[:, at : at + rows].T * factor).astype(d_ref.dtype)
            at += peers * rows
            back_ref[block, which] = (acc[:, at : at + rows].T * factor).astype(back_ref.dtype)


def attention(bias, qg, own, prev, head, *held):
    peers, _, _, rows, _ = own.shape
    width = 2 * peers * rows
    whole = pl.BlockSpec(prev.shape, lambda i: (0, 0, 0, 0))
    slot = pl.BlockSpec((peers, 1, 2, rows, HEAD), lambda i: (0, head, 0, 0, 0))
    both = pltpu.HBM(own.shape, own.dtype)
    return pl.pallas_call(
        attention_kernel,
        grid=(1,),
        in_specs=[pl.BlockSpec((1, width // 2 // CH, width), lambda i: (0, 0, 0)), slot, slot, whole]
        + [pl.BlockSpec(memory_space=pl.ANY)] * len(held),
        out_specs=(slot, slot, whole),
        out_shape=(both, both, jax.ShapeDtypeStruct(prev.shape, prev.dtype)),
        input_output_aliases={4 + n: n for n in range(len(held))},
        scratch_shapes=[pltpu.VMEM((HEAD, width), jnp.float32)] * 2 + [pltpu.VMEM((2, TILE, width), jnp.float32)] * 2,
        compiler_params=pltpu.CompilerParams(vmem_limit_bytes=48 * 2**20),
        cost_estimate=pl.CostEstimate(flops=12 * 10**9, bytes_accessed=4 * 2**20, transcendentals=2 * 2**20),
    )(bias, qg, own, prev, *held)


def window_bias(stretch_pos, block_mask, group, groups, span):
    prev = (group + groups - 1) % groups
    own_pos = lax.dynamic_slice_in_dim(stretch_pos, group * span, span, 0)
    prev_pos = lax.dynamic_slice_in_dim(stretch_pos, prev * span, span, 0)
    key_pos = jnp.concatenate([own_pos, prev_pos], axis=0)
    flags = lax.dynamic_slice_in_dim(block_mask, group * span, span, 0)
    seen = jnp.logical_and(flags == 1, key_pos[None, :] <= own_pos[:, None])
    bias = jnp.where(seen, 0.0, NEG).astype(jnp.float32)
    wide = jnp.broadcast_to(bias[:, :, None], bias.shape + (CH,))
    return wide.reshape(1, span, -1)


def hop(value, pairs, count):
    flat = [(i * count + s, j * count + d) for (s, i), (d, j) in pairs]
    return lax.ppermute(value, ("inner", "outer"), flat)


def routes(steps, relay, count, peers):
    edge, entry = (RUN - 1, 0) if steps == 1 else (0, RUN - 1)
    within, direct, second = [], [], []
    for s in range(count):
        for i in range(peers):
            to = (s + steps) % count
            if s % RUN != edge:
                within.append(((s, i), (to, i)))
            elif i in relay:
                near = s // RUN * RUN + entry
                within.append(((s, i), (near, i)))
                second.append(((near, i), (to, i)))
            else:
                direct.append(((s, i), (to, i)))
    return within, direct, second


def sent(value, steps, relay):
    count, peers = lax.axis_size("outer"), lax.axis_size("inner")
    within, direct, second = routes(steps, relay, count, peers)
    across = hop(value, direct, count) if direct else None

    def finish(near):
        far = hop(near, second, count) if second else across
        if direct and second:
            inner = lax.axis_index("inner")
            far = jnp.where(jnp.logical_and(inner >= relay[0], inner <= relay[-1]), far, across)
        return jnp.where(lax.axis_index("outer") % RUN == (0 if steps == 1 else RUN - 1), far, near)

    return hop(value, within, count), finish


def shifted(value, steps):
    count = lax.axis_size("outer")
    return lax.ppermute(value, "outer", [(s, (s + steps) % count) for s in range(count)])


def after(value, *earlier):
    return lax.optimization_barrier((value, *earlier))


def add_at(d, head, back):
    own = lax.index_in_dim(d, head, 1, keepdims=False)
    return lax.dynamic_update_slice_in_dim(d, added(own, back)[:, None], head, axis=1)


def body(queries, keys, values, out_grad, stretch_pos, block_mask):
    peers = lax.axis_size("inner")
    groups = lax.axis_size("outer")
    bias = window_bias(stretch_pos, block_mask, lax.axis_index("outer"), groups, 2 * peers)
    upper = range(peers // 2, peers)
    kv = exchanged(pack(keys, values, peers))
    kv0, kv1, qg = lax.optimization_barrier((kv[:, 0], kv[:, 1], pack(queries, out_grad, peers)))
    near, finish = sent(kv0, 1, upper)
    kv1, near = after(kv1, near)
    prev_kv1 = shifted(kv1, 1)
    qg = exchanged(qg)
    prev_kv0 = finish(near)
    oq, d, back0 = attention(bias, qg, kv, prev_kv0, 0)
    back0 = shifted(back0, -1)
    oq, d, back1 = attention(bias, qg, kv, prev_kv1, 1, oq, d)
    back1, back0 = after(back1, back0)
    near, finish = sent(back1, -1, upper)
    oq = exchanged(oq)
    d = add_at(d, 0, back0)
    d = add_at(d, 1, finish(near))
    d, oq = after(d, oq)
    output, dquery = unpack(oq)
    d_key, d_value = unpack(exchanged(d))
    return (output, dquery, d_key, d_value)


def solution(mesh):
    rows = P(("outer", "inner"), None)
    return jax.shard_map(
        body,
        mesh=mesh,
        in_specs=(rows, rows, rows, rows, P(), P()),
        out_specs=(rows, rows, rows, rows),
        check_vma=False,
    )
```

```python
import jax
import jax.numpy as jnp
from jax import lax
from jax.experimental import pallas as pl
from jax.experimental.pallas import tpu as pltpu
from jax.sharding import PartitionSpec as P

H = 16
HEAD = 128
CH = 64
NEG = -1e30
TILE = 256
SCALE = 1.0 / HEAD**0.5
LOG2E = 1.4426950408889634
RUN = 8


def exchanged(value):
    return lax.all_to_all(value, "inner", split_axis=0, concat_axis=0, tiled=True)


def added(a, b):
    return (a.astype(jnp.float32) + b.astype(jnp.float32)).astype(jnp.bfloat16)


def dot(a, b):
    return lax.dot_general(a, b, (((1,), (0,)), ((), ())), preferred_element_type=jnp.float32)


def dot_t(a, b):
    return lax.dot_general(a, b, (((1,), (1,)), ((), ())), preferred_element_type=jnp.float32)


def pack_kernel(a_ref, b_ref, o_ref):
    peers, heads = o_ref.shape[:2]
    for at in range(peers * heads):
        for which, ref in enumerate((a_ref, b_ref)):
            o_ref[at // heads, at % heads, which] = ref[:, at * HEAD : (at + 1) * HEAD]


def pack(a, b, peers):
    rows, width = a.shape
    heads = width // HEAD // peers
    part = pl.BlockSpec((rows, width // 2), lambda i: (0, i))
    return pl.pallas_call(
        pack_kernel,
        grid=(2,),
        in_specs=[part, part],
        out_specs=pl.BlockSpec((peers // 2, heads, 2, rows, HEAD), lambda i: (i, 0, 0, 0, 0)),
        out_shape=pltpu.HBM((peers, heads, 2, rows, HEAD), a.dtype),
    )(a, b)


def unpack_kernel(i_ref, a_ref, b_ref, va, vb, come, go):
    peers, heads = i_ref.shape[:2]
    held = []
    for which, to in enumerate((va, vb)):
        for at in range(peers * heads):
            part = i_ref.at[at // heads, at % heads, which]
            held.append(pltpu.make_async_copy(part, to.at[:, pl.ds(at * HEAD, HEAD)], come.at[at, which]))
            held[-1].start()
    for copy in held:
        copy.wait()
    held = [pltpu.make_async_copy(x, y, go.at[n]) for n, (x, y) in enumerate(((va, a_ref), (vb, b_ref)))]
    for copy in held:
        copy.start()
    for copy in held:
        copy.wait()


def unpack(packed):
    peers, heads, _, rows, _ = packed.shape
    shape = pltpu.HBM((rows, peers * heads * HEAD), packed.dtype)
    room = pltpu.VMEM((rows, peers * heads * HEAD), packed.dtype)
    return pl.pallas_call(
        unpack_kernel,
        out_shape=(shape, shape),
        in_specs=[pl.BlockSpec(memory_space=pl.ANY)],
        out_specs=(pl.BlockSpec(memory_space=pltpu.HBM),) * 2,
        scratch_shapes=[room, room, pltpu.SemaphoreType.DMA((peers * heads, 2)), pltpu.SemaphoreType.DMA((2,))],
        compiler_params=pltpu.CompilerParams(vmem_limit_bytes=48 * 2**20),
    )(packed)


def attend(bias_ref, qg_ref, keys, vals, put, acc_k, acc_v, s_ref, dp_ref, p_ref):
    span = keys[0].shape[0]
    rows = qg_ref.shape[3]
    per = TILE // rows
    row = lax.broadcasted_iota(jnp.int32, (TILE, TILE), 0)
    col = lax.broadcasted_iota(jnp.int32, (TILE, TILE), 1)
    later = jnp.where(jnp.logical_and(row // CH == col // CH, col > row), NEG, 0.0)
    halves = [slice(half * span, (half + 1) * span) for half in range(2)]

    def scores(tile):
        q = qg_ref[tile * per : (tile + 1) * per, 0, 0].reshape(TILE, HEAD)
        g = qg_ref[tile * per : (tile + 1) * per, 0, 1].reshape(TILE, HEAD)
        own = slice(tile * TILE, (tile + 1) * TILE)
        for half, cols in enumerate(halves):
            seen = [bias_ref[0, at // CH : at // CH + 1, cols] for at in range(own.start, own.stop, CH)]
            seen = jnp.concatenate([jnp.broadcast_to(line, (CH, span)) for line in seen], axis=0)
            s = dot_t(q, keys[half]) * (SCALE * LOG2E) + seen
            if half == 0:
                parts = (s[:, : own.start], s[:, own] + later, s[:, own.stop :])
                s = jnp.concatenate([part for part in parts if part.shape[1]], axis=1)
            s_ref[tile % 2, :, cols] = s
            dp_ref[tile % 3, :, cols] = dot_t(g, vals[half])
        return q, g

    def soften(tile):
        s = s_ref[tile % 2]
        top = jnp.max(s, axis=1, keepdims=True)
        e = jnp.exp2(s - top)
        total = jnp.sum(e, axis=1, keepdims=True)
        p_ref[tile % 2] = e * (1.0 / total)

    def finish(tile, q, g):
        p = p_ref[tile % 2]
        pb = p.astype(jnp.bfloat16)
        out = (dot(pb[:, halves[0]], vals[0]) + dot(pb[:, halves[1]], vals[1])).astype(jnp.bfloat16)
        delta = jnp.sum(g.astype(jnp.float32) * out.astype(jnp.float32), axis=1, keepdims=True)
        dq = jnp.zeros((TILE, HEAD), jnp.float32)
        qt, gt = q.T, g.T
        for half, cols in enumerate(halves):
            ds = (p[:, cols] * (dp_ref[tile % 3, :, cols] - delta)).astype(jnp.bfloat16)
            dq = dq + dot(ds, keys[half])
            for acc, term in ((acc_k, dot(qt, ds)), (acc_v, dot(gt, pb[:, cols]))):
                acc[:, cols] = term if tile == 0 else acc[:, cols] + term
        put(slice(tile * per, (tile + 1) * per), out, (dq * SCALE).astype(jnp.bfloat16))

    tiles = span // TILE
    rows_of = {}
    for step in range(tiles + 2):
        if step < tiles:
            rows_of[step] = scores(step)
        if 0 <= step - 1 < tiles:
            soften(step - 1)
        if 0 <= step - 2 < tiles:
            finish(step - 2, *rows_of[step - 2])


def attention_kernel(bias_ref, qg_ref, own_ref, prev_ref, *rest):
    oq_ref, d_ref, back_ref = rest[-8:-5]
    scratch = rest[-5:]
    peers, _, rows, _ = prev_ref.shape

    def put(blocks, out, dq):
        for which, value in ((0, out), (1, dq)):
            oq_ref[blocks, 0, which] = value.reshape(-1, rows, HEAD)

    keys, vals = ((own_ref[:, 0, w].reshape(-1, HEAD), prev_ref[:, w].reshape(-1, HEAD)) for w in range(2))
    attend(bias_ref, qg_ref, keys, vals, put, *scratch)
    for which, acc, factor in ((0, scratch[0], SCALE), (1, scratch[1], 1.0)):
        for block in range(peers):
            at = block * rows
            d_ref[block, 0, which] = (acc[:, at : at + rows].T * factor).astype(d_ref.dtype)
            at += peers * rows
            back_ref[block, which] = (acc[:, at : at + rows].T * factor).astype(back_ref.dtype)


def attention(bias, qg, own, prev, head, *held):
    peers, _, _, rows, _ = own.shape
    width = 2 * peers * rows
    whole = pl.BlockSpec(prev.shape, lambda i: (0, 0, 0, 0))
    slot = pl.BlockSpec((peers, 1, 2, rows, HEAD), lambda i: (0, head, 0, 0, 0))
    both = pltpu.HBM(own.shape, own.dtype)
    return pl.pallas_call(
        attention_kernel,
        grid=(1,),
        in_specs=[pl.BlockSpec((1, width // 2 // CH, width), lambda i: (0, 0, 0)), slot, slot, whole]
        + [pl.BlockSpec(memory_space=pl.ANY)] * len(held),
        out_specs=(slot, slot, whole),
        out_shape=(both, both, jax.ShapeDtypeStruct(prev.shape, prev.dtype)),
        input_output_aliases={4 + n: n for n in range(len(held))},
        scratch_shapes=[pltpu.VMEM((HEAD, width), jnp.float32)] * 2 + [pltpu.VMEM((n, TILE, width), jnp.float32) for n in (2, 3, 2)],
        compiler_params=pltpu.CompilerParams(vmem_limit_bytes=48 * 2**20),
        cost_estimate=pl.CostEstimate(flops=12 * 10**9, bytes_accessed=4 * 2**20, transcendentals=2 * 2**20),
    )(bias, qg, own, prev, *held)


def window_bias(stretch_pos, block_mask, group, groups, span):
    prev = (group + groups - 1) % groups
    own_pos = lax.dynamic_slice_in_dim(stretch_pos, group * span, span, 0)
    prev_pos = lax.dynamic_slice_in_dim(stretch_pos, prev * span, span, 0)
    key_pos = jnp.concatenate([own_pos, prev_pos], axis=0)
    flags = lax.dynamic_slice_in_dim(block_mask, group * span, span, 0)
    seen = jnp.logical_and(flags == 1, key_pos[None, :] <= own_pos[:, None])
    bias = jnp.where(seen, 0.0, NEG).astype(jnp.float32)
    wide = jnp.broadcast_to(bias[:, :, None], bias.shape + (CH,))
    return wide.reshape(1, span, -1)


def hop(value, pairs, count):
    flat = [(i * count + s, j * count + d) for (s, i), (d, j) in pairs]
    return lax.ppermute(value, ("inner", "outer"), flat)


def routes(steps, relay, count, peers):
    edge, entry = (RUN - 1, 0) if steps == 1 else (0, RUN - 1)
    within, direct, second = [], [], []
    for s in range(count):
        for i in range(peers):
            to = (s + steps) % count
            if s % RUN != edge:
                within.append(((s, i), (to, i)))
            elif i in relay:
                near = s // RUN * RUN + entry
                within.append(((s, i), (near, i)))
                second.append(((near, i), (to, i)))
            else:
                direct.append(((s, i), (to, i)))
    return within, direct, second


def sent(value, steps, relay):
    count, peers = lax.axis_size("outer"), lax.axis_size("inner")
    within, direct, second = routes(steps, relay, count, peers)
    across = hop(value, direct, count) if direct else None

    def finish(near):
        far = hop(near, second, count) if second else across
        if direct and second:
            inner = lax.axis_index("inner")
            far = jnp.where(jnp.logical_and(inner >= relay[0], inner <= relay[-1]), far, across)
        return jnp.where(lax.axis_index("outer") % RUN == (0 if steps == 1 else RUN - 1), far, near)

    return hop(value, within, count), finish


def shifted(value, steps):
    count = lax.axis_size("outer")
    return lax.ppermute(value, "outer", [(s, (s + steps) % count) for s in range(count)])


def after(value, *earlier):
    return lax.optimization_barrier((value, *earlier))


def add_at(d, head, back):
    own = lax.index_in_dim(d, head, 1, keepdims=False)
    return lax.dynamic_update_slice_in_dim(d, added(own, back)[:, None], head, axis=1)


def body(queries, keys, values, out_grad, stretch_pos, block_mask):
    peers = lax.axis_size("inner")
    groups = lax.axis_size("outer")
    bias = window_bias(stretch_pos, block_mask, lax.axis_index("outer"), groups, 2 * peers)
    upper = range(peers // 2, peers)
    kv = exchanged(pack(keys, values, peers))
    kv0, kv1, qg = lax.optimization_barrier((kv[:, 0], kv[:, 1], pack(queries, out_grad, peers)))
    near, finish = sent(kv0, 1, upper)
    kv1, near = after(kv1, near)
    prev_kv1 = shifted(kv1, 1)
    qg = exchanged(qg)
    prev_kv0 = finish(near)
    oq, d, back0 = attention(bias, qg, kv, prev_kv0, 0)
    back0 = shifted(back0, -1)
    oq, d, back1 = attention(bias, qg, kv, prev_kv1, 1, oq, d)
    back1, back0 = after(back1, back0)
    near, finish = sent(back1, -1, upper)
    oq = exchanged(oq)
    d = add_at(d, 0, back0)
    d = add_at(d, 1, finish(near))
    d, oq = after(d, oq)
    output, dquery = unpack(oq)
    d_key, d_value = unpack(exchanged(d))
    return (output, dquery, d_key, d_value)


def solution(mesh):
    rows = P(("outer", "inner"), None)
    return jax.shard_map(
        body,
        mesh=mesh,
        in_specs=(rows, rows, rows, rows, P(), P()),
        out_specs=(rows, rows, rows, rows),
        check_vma=False,
    )
```
